512 devices in a mesh: dx: 16 (over y, z_lo), dy: 32 (over z_hi, x, core).
Axes of the slice: x: 4, y: 4, z: 16 (z_hi: 4, z_lo: 4; z = z_hi * 4 + z_lo), core: 2. Of those that a mesh axis runs over, the one named last changes fastest.
Arguments:
- images: float32 [131072, 1152], P(('dx', 'dy')), may hold values from -1 to 1
- texts: float32 [131072, 1152], P(('dx', 'dy')), may hold values from -1 to 1
- match: int32 [512, 256], P(('dx', 'dy')), may hold values from 0 to 255, each once within a row
- masks: int32 [3], replicated, may hold values from 1 to 256, as said below
Outputs:
- image_grad: float32 [131072, 1152], P(('dx', 'dy'))
- text_grad: float32 [131072, 1152], P(('dx', 'dy'))
- block_loss: float32 [512], P(('dx', 'dy'))
The draws below stay inside these ranges and needn't reach their ends.
Inputs may be any that keep to these rules, and one draw needn't show every extreme that they name: `masks`: each entry is a power of two below 512 and the entries differ; the first is below 32, the second is 256.
All inputs are finite; a program needn't handle non-finite values.
Results may differ from the reference program's by a relative error of at most 0.0045.
Values may be sent and summed in bfloat16 or wider, within the bound.
A program may use at most 64 MiB of HBM per device.

```python
import jax
import jax.numpy as jnp
from jax import lax

D = 1152
B = 256
ROUNDS = 3
BLOCKS = 512
PAIRS = 131072
N_DY = 32


def draw_masks(key, part):
    key = jax.random.fold_in(key, 7)
    low_bits = N_DY.bit_length() - 1
    all_bits = BLOCKS.bit_length() - 1
    first_key, third_key = jax.random.split(key, 2)
    first = jax.random.randint(first_key, (1,), 0, low_bits)
    second = jnp.full((1,), all_bits - 1, jnp.int32)
    order = jax.random.permutation(third_key, all_bits)
    usable = jnp.logical_and(order[None, :] != first[:, None], order[None, :] != second[:, None])
    rank = jnp.arange(all_bits)
    score = jnp.where(usable[0], all_bits - rank, -1)
    taken = jnp.zeros((all_bits,), jnp.int32)
    chosen = []
    for slot in range(ROUNDS - 2):
        pick = jnp.argmax(jnp.where(taken > 0, -1, score))
        taken = taken.at[pick].set(1)
        chosen.append(order[pick][None])
    bits = jnp.concatenate([first.astype(jnp.int32), second] + [c.astype(jnp.int32) for c in chosen]).astype(jnp.int32)
    return jnp.left_shift(jnp.ones_like(bits), bits).astype(jnp.int32)


def block_levels(stream_key, extent, shards, smallest, top_value):
    loudness = 1.0
    for axis_at, shards_of in shards:
        steps = jax.random.uniform(jax.random.fold_in(jax.random.fold_in(stream_key, 6), axis_at), (shards_of,), jnp.float32, smallest / len(shards), top_value / len(shards))
        loudness = loudness * jnp.repeat(jnp.exp(steps), extent[axis_at] // shards_of).reshape((-1,) + (1,) * (len(extent) - 1 - axis_at))
    return loudness


def normal_values(rng, dims, spread, bound, cuts=(), kind=jnp.bfloat16):
    result = jax.random.normal(rng, dims, jnp.float32) * spread
    if len(cuts) > 0:
        result = block_levels(rng, dims, cuts, -0.22, 0.18) * result
    return jnp.clip(result, min=-bound, max=bound).astype(kind)


def setup_inputs(seed: int = 0) -> dict:
    arg_keys = jax.random.split(jax.random.key(seed), 5)
    return {
        "images": normal_values(arg_keys[0], (PAIRS, D), (D // 32) ** -0.5, 1.0, ((0, 512),), jnp.float32),
        "texts": normal_values(arg_keys[1], (PAIRS, D), (D // 32) ** -0.5, 1.0, ((0, 512),), jnp.float32),
        "match": jax.vmap(lambda own: jax.random.permutation(own, B))(jax.random.split(arg_keys[2], BLOCKS)).reshape((BLOCKS, B)).astype(jnp.int32),
        "masks": draw_masks(jax.random.fold_in(arg_keys[4], 71), 0),
    }


bias_value = -2.0


def met_tile(img_block, txt_block, labels):
    logits = jnp.dot(img_block, txt_block.T, preferred_element_type=jnp.float32) + bias_value
    loss = jnp.sum(jax.nn.softplus(-(2.0 * labels - 1.0) * logits))
    g = (jax.nn.sigmoid(logits) - labels).astype(jnp.bfloat16)
    image_term = jnp.dot(g, txt_block, preferred_element_type=jnp.float32)
    text_term = jnp.dot(g.T, img_block, preferred_element_type=jnp.float32)
    return image_term, text_term, loss


def reference(images, texts, match, masks):
    img = images.astype(jnp.bfloat16).reshape(BLOCKS, B, D)
    txt = texts.astype(jnp.bfloat16).reshape(BLOCKS, B, D)
    column = lax.broadcasted_iota(jnp.int32, (B, B), 1)
    blocks = jnp.arange(BLOCKS, dtype=jnp.int32)

    def own(index):
        labels = (column == match[index][:, None]).astype(jnp.float32)
        return met_tile(img[index], txt[index], labels)

    image_grad, text_grad, losses = lax.map(own, blocks)
    zeros = jnp.zeros((B, B), jnp.float32)
    for r in range(ROUNDS):
        partner = jnp.bitwise_xor(blocks, masks[r]).astype(jnp.int32)

        def visit(index):
            return met_tile(img[index], txt[partner[index]], zeros)

        image_term, text_term, loss = lax.map(visit, blocks)
        image_grad = image_grad + image_term
        text_grad = text_grad + text_term[partner]
        losses = losses + loss
    block_loss = losses / (B * B * (ROUNDS + 1.0))
    return image_grad.reshape(PAIRS, D), text_grad.reshape(PAIRS, D), block_loss
```

```python
from functools import partial

import jax
import jax.numpy as jnp
from jax import lax
from jax.experimental import pallas as pl
from jax.experimental.pallas import tpu as pltpu
from jax.sharding import PartitionSpec as P

MESH = pl.DeviceIdType.MESH
BIAS = -2.0
CHUNK = 32

SECOND = 8
FAR = {8: (7,), 2: (1,), 4: (3, 6, 5)}


def plan_for(bits):
    place_of = {bit: ("recv", slot) for slot, bit in enumerate(bits)}
    relays = 0
    streams = []
    forwards = []
    for bit in (4, 8, 2):
        if bit not in bits:
            continue
        near = next((b for b in FAR[bit] if b in bits), None)
        if near is None:
            near = FAR[bit][-1]
            place_of[near] = ("relay", relays)
            relays += 1
        forwards.append((near, bit))
    for near, _ in forwards:
        streams.append((1 << near, place_of[near]))
    forwarded = {near for near, _ in forwards}
    reached = {far for _, far in forwards}
    for bit in bits:
        if bit not in forwarded and bit not in reached:
            streams.append((1 << bit, place_of[bit]))
    hops = [
        (streams.index((1 << near, place_of[near])), 1 << near | 1 << far, place_of[far])
        for near, far in forwards
    ]
    return streams, hops, relays


def exchange(streams, hops, low_count, images_ref, texts_ref, recv, own, relay, send_sem, recv_sem):
    dx, dy = lax.axis_index("dx"), lax.axis_index("dy")

    def flipped(index, mask):
        for k in range(16):
            if mask >> k & 1:
                step = 1 << k
                index = index + step * (1 - 2 * ((index // step) % 2))
        return index

    def device(mask):
        return (flipped(dx, mask // low_count), flipped(dy, mask % low_count))

    targets = [mask for mask, _ in streams] + [mask for _, mask, _ in hops]
    barrier = pltpu.get_barrier_semaphore()
    for mask in targets:
        pl.semaphore_signal(barrier, inc=1, device_id=device(mask), device_id_type=MESH)
    half = texts_ref.shape[0]
    own[pl.ds(0, half), :] = texts_ref[...].astype(jnp.bfloat16)
    own[pl.ds(half, half), :] = images_ref[...].astype(jnp.bfloat16)
    pl.semaphore_wait(barrier, len(targets))

    buffers = {"recv": recv, "relay": relay}

    def ref_of(place):
        return buffers[place[0]].at[place[1]]

    def copy(index, source, place, mask, chunk):
        rows = pl.ds(pl.multiple_of(chunk * CHUNK, CHUNK), CHUNK)
        return pltpu.make_async_remote_copy(
            src_ref=source.at[rows],
            dst_ref=ref_of(place).at[rows],
            send_sem=send_sem.at[index, chunk],
            recv_sem=recv_sem.at[index, chunk],
            device_id=device(mask),
            device_id_type=MESH,
        )

    def first(index, chunk):
        mask, place = streams[index]
        return copy(index, own, place, mask, chunk)

    def second(index, chunk):
        via, mask, place = hops[index]
        return copy(len(streams) + index, ref_of(streams[via][1]), place, mask, chunk)

    chunks = 2 * half // CHUNK

    @pl.loop(0, chunks)
    def _(chunk):
        for index in range(len(streams)):
            first(index, chunk).start()

    @pl.loop(0, chunks)
    def _(chunk):
        for index in range(len(hops)):
            first(hops[index][0], chunk).wait_recv()
            second(index, chunk).start()

    vias = {via for via, _, _ in hops}

    @pl.loop(0, chunks)
    def _(chunk):
        for index in range(len(streams)):
            first(index, chunk).wait_send()
            if index not in vias:
                first(index, chunk).wait_recv()
        for index in range(len(hops)):
            second(index, chunk).wait()


def exchange_call(bits, number, low_count, images, texts):
    half, width = images.shape
    streams, hops, relays = plan_for(bits)
    chunks = 2 * half // CHUNK
    total = len(streams) + len(hops)
    return pl.pallas_call(
        partial(exchange, streams, hops, low_count),
        out_shape=jax.ShapeDtypeStruct((len(bits), 2 * half, width), jnp.bfloat16),
        in_specs=[pl.BlockSpec(memory_space=pltpu.VMEM)] * 2,
        out_specs=pl.BlockSpec(memory_space=pl.ANY),
        scratch_shapes=[
            pltpu.VMEM((2 * half, width), jnp.bfloat16),
            pltpu.VMEM((max(relays, 1), 2 * half, width), jnp.bfloat16),
            pltpu.SemaphoreType.DMA((total, chunks)),
            pltpu.SemaphoreType.DMA((total, chunks)),
        ],
        compiler_params=pltpu.CompilerParams(
            collective_id=number, has_side_effects=True, vmem_limit_bytes=32 * 2**20
        ),
        name="exchange_" + "_".join(str(bit) for bit in bits),
    )(images, texts)


def across(a, b):
    return lax.dot_general(a, b, (((1,), (1,)), ((), ())), preferred_element_type=jnp.float32)


def sigmoid_parts(logits):
    e = jnp.exp(-jnp.abs(logits))
    return jnp.where(logits >= 0, 1.0, e) / (1.0 + e), e


def tiles(scale, images_ref, texts_ref, match_ref, recv, image_grad, text_grad, loss_ref, own):
    step = pl.program_id(0)
    half = texts_ref.shape[0]

    @pl.when(step == 0)
    def _():
        txt = texts_ref[...].astype(jnp.bfloat16)
        img = images_ref[...].astype(jnp.bfloat16)
        own[0] = txt
        own[1] = img
        logits = across(txt, img) + BIAS
        row = lax.broadcasted_iota(jnp.int32, logits.shape, 0)
        hit = row == match_ref[...]
        s, e = sigmoid_parts(logits)
        g = (s - jnp.where(hit, 1.0, 0.0)).astype(jnp.bfloat16)
        loss = jnp.maximum(jnp.where(hit, -logits, logits), 0.0) + jnp.log1p(e)
        loss_ref[0] = jnp.sum(loss) * scale
        text_grad[...] = jnp.dot(g, img, preferred_element_type=jnp.float32)
        image_grad[...] = lax.dot_general(
            g, txt, (((0,), (0,)), ((), ())), preferred_element_type=jnp.float32
        )

    @pl.when(step > 0)
    def _():
        other_txt = recv[0, pl.ds(0, half), :]
        logits = across(own[1], other_txt) + BIAS
        s, e = sigmoid_parts(logits)
        loss_ref[0] += jnp.sum(jnp.maximum(logits, 0.0) + jnp.log1p(e)) * scale
        image_grad[...] += jnp.dot(
            s.astype(jnp.bfloat16), other_txt, preferred_element_type=jnp.float32
        )
        other_img = recv[0, pl.ds(half, half), :]
        s, _ = sigmoid_parts(across(own[0], other_img) + BIAS)
        text_grad[...] += jnp.dot(
            s.astype(jnp.bfloat16), other_img, preferred_element_type=jnp.float32
        )


def tiles_call(images, texts, match, recv):
    half, width = images.shape
    rounds = recv.shape[0]
    whole = pl.BlockSpec((half, width), lambda i: (0, 0))
    grad = jax.ShapeDtypeStruct((half, width), jnp.float32)
    flops = 2 * half * half * width * (3 + 4 * rounds)
    return pl.pallas_call(
        partial(tiles, 1.0 / (half * half * (rounds + 1.0))),
        grid=(rounds + 1,),
        out_shape=(grad, grad, jax.ShapeDtypeStruct((1,), jnp.float32)),
        in_specs=[
            whole,
            whole,
            pl.BlockSpec((1, half), lambda i: (0, 0)),
            pl.BlockSpec((1, 2 * half, width), lambda i: (jnp.maximum(i - 1, 0), 0, 0)),
        ],
        out_specs=(whole, whole, pl.BlockSpec(memory_space=pltpu.SMEM)),
        scratch_shapes=[pltpu.VMEM((2, half, width), jnp.bfloat16)],
        compiler_params=pltpu.CompilerParams(vmem_limit_bytes=40 * 2**20),
        cost_estimate=pl.CostEstimate(
            flops=flops, bytes_accessed=16 * half * width + recv.size * 2, transcendentals=0
        ),
        name="tiles",
    )(images, texts, match, recv)


def body(low_count, all_bits, images, texts, match, masks):
    low_bits = low_count.bit_length() - 1
    sets, number = [], {}
    table = []
    for one in range(all_bits):
        for other in range(all_bits):
            low, high = min(one, other), max(one, other)
            if low == high or low >= low_bits or SECOND in (low, high):
                table.append(0)
                continue
            if (low, high) not in number:
                number[low, high] = len(sets)
                sets.append((low, high, SECOND))
            table.append(number[low, high])
    bit = jnp.sum((masks[:, None] >= (1 << jnp.arange(1, all_bits))[None, :]).astype(jnp.int32), 1)
    index = jnp.array(table, jnp.int32)[bit[0] * all_bits + bit[2]]
    branches = [
        partial(exchange_call, bits, at, low_count) for at, bits in enumerate(sets)
    ]
    recv = lax.switch(index, branches, images, texts)
    return tiles_call(images, texts, match, recv)


def solution(mesh):
    rows = P(("dx", "dy"), None)
    low_count = mesh.shape["dy"]
    all_bits = (low_count * mesh.shape["dx"]).bit_length() - 1
    return jax.shard_map(
        partial(body, low_count, all_bits),
        mesh=mesh,
        in_specs=(rows, rows, rows, P()),
        out_specs=(rows, rows, P(("dx", "dy"))),
        check_vma=False,
    )
```

```python
from functools import partial

import jax
import jax.numpy as jnp
from jax import lax
from jax.experimental import pallas as pl
from jax.experimental.pallas import tpu as pltpu
from jax.sharding import PartitionSpec as P

BIAS = -2.0
SECOND = 8
BLOCKS_OF_ROWS = 2

LOAD = {0: 0.2, 1: 1, 2: 1.01, 3: 4, 4: 4.01, 5: 1, 6: 2, 7: 1, 8: 1.02}
RELAYED = {(1, 2), (3, 4), (4, 5), (4, 6), (7, 8)}
PIECES = 4


def across(a, b):
    return lax.dot_general(a, b, (((1,), (1,)), ((), ())), preferred_element_type=jnp.float32)


def times(a, b):
    return jnp.dot(a, b, preferred_element_type=jnp.float32)


def sigmoid_parts(logits):
    e = jnp.exp(-jnp.abs(logits))
    return jnp.where(logits >= 0, 1.0, e) / (1.0 + e), e


def params():
    return pltpu.CompilerParams(vmem_limit_bytes=40 * 2**20)


def prepare(all_bits, masks_ref, images_ref, texts_ref, img_ref, txt_ref, both_ref, index_ref):
    txt_ref[...] = both_ref[0] = texts_ref[...].astype(jnp.bfloat16)
    img_ref[...] = both_ref[1] = images_ref[...].astype(jnp.bfloat16)
    first, third = masks_ref[0], masks_ref[2]
    low, high = jnp.minimum(first, third), jnp.maximum(first, third)
    low_bit, high_bit = jnp.int32(0), jnp.int32(0)
    for k in range(1, all_bits):
        low_bit += (low >= 1 << k).astype(jnp.int32)
        high_bit += (high >= 1 << k).astype(jnp.int32)
    others = all_bits - 1
    before = low_bit * others - low_bit * (low_bit + 1) // 2
    index_ref[0] = before + high_bit - low_bit - 1


def prepare_call(all_bits, masks, images, texts):
    half, width = images.shape
    rows = half // BLOCKS_OF_ROWS
    block = pl.BlockSpec((rows, width), lambda i: (i, 0))
    short = jax.ShapeDtypeStruct((half, width), jnp.bfloat16)
    pair = jax.ShapeDtypeStruct((2, half, width), jnp.bfloat16)
    smem = pl.BlockSpec(memory_space=pltpu.SMEM)
    return pl.pallas_call(
        partial(prepare, all_bits),
        grid=(BLOCKS_OF_ROWS,),
        out_shape=(short, short, pair, jax.ShapeDtypeStruct((1,), jnp.int32)),
        in_specs=[smem, block, block],
        out_specs=(block, block, pl.BlockSpec((2, rows, width), lambda i: (0, i, 0)), smem),
        compiler_params=params(),
        name="prepare",
    )(masks, images, texts)


def own_tile(scale, img_ref, txt_ref, match_ref, image_ref, text_ref, loss_ref):
    txt, img = txt_ref[...], img_ref[...]
    logits = across(txt, img) + BIAS
    row = lax.broadcasted_iota(jnp.int32, logits.shape, 0)
    hit = row == match_ref[...]
    s, e = sigmoid_parts(logits)
    g = (s - jnp.where(hit, 1.0, 0.0)).astype(jnp.bfloat16)
    loss = jnp.maximum(jnp.where(hit, -logits, logits), 0.0) + jnp.log1p(e)
    loss_ref[0] = jnp.sum(loss) * scale
    text_ref[...] = times(g, img)
    image_ref[...] = lax.dot_general(
        g, txt, (((0,), (0,)), ((), ())), preferred_element_type=jnp.float32
    )


def own_call(scale, img, txt, match):
    half, width = img.shape
    grad = jax.ShapeDtypeStruct((half, width), jnp.float32)
    vmem = pl.BlockSpec(memory_space=pltpu.VMEM)
    return pl.pallas_call(
        partial(own_tile, scale),
        out_shape=(grad, grad, jax.ShapeDtypeStruct((1,), jnp.float32)),
        in_specs=[vmem, vmem, vmem],
        out_specs=(vmem, vmem, pl.BlockSpec(memory_space=pltpu.SMEM)),
        compiler_params=params(),
        cost_estimate=pl.CostEstimate(
            flops=6 * half * half * width, bytes_accessed=12 * half * width, transcendentals=0
        ),
        name="own_tile",
    )(img, txt, match)


def add_term(scale, pieces, *refs):
    mine_ref, refs = refs[0], refs[1:]
    others, refs = refs[:pieces], refs[pieces:]
    if scale is None:
        sum_ref, out_ref = refs
    else:
        sum_ref, before_ref, out_ref, loss_ref = refs
    mine = mine_ref[...]
    total = sum_ref[...]
    losses = []
    for other_ref in others:
        other = other_ref[...].reshape(other_ref.shape[-2:])
        logits = across(mine, other) + BIAS
        s, e = sigmoid_parts(logits)
        total = total + times(s.astype(jnp.bfloat16), other)
        if scale is not None:
            losses.append(jnp.sum(jnp.maximum(logits, 0.0) + jnp.log1p(e)))
    out_ref[...] = total
    if scale is not None:

        @pl.when(pl.program_id(0) == 0)
        def _():
            loss_ref[0] = before_ref[0]

        loss_ref[0] += sum(losses) * scale


def add_call(scale, mine, others, total, loss=None):
    half, width = mine.shape
    rows = half // BLOCKS_OF_ROWS
    block = pl.BlockSpec((rows, width), lambda i: (i, 0))
    whole = [
        pl.BlockSpec(other.shape, lambda i: (0, 0))
        if at is None
        else pl.BlockSpec((1, *other.shape[1:]), lambda i, at=at: (at, 0, 0))
        for other, at in others
    ]
    smem = pl.BlockSpec(memory_space=pltpu.SMEM)
    grad = jax.ShapeDtypeStruct((half, width), jnp.float32)
    count = len(others)
    with_loss = loss is not None
    return pl.pallas_call(
        partial(add_term, scale if with_loss else None, count),
        grid=(BLOCKS_OF_ROWS,),
        out_shape=(grad, jax.ShapeDtypeStruct((1,), jnp.float32)) if with_loss else grad,
        in_specs=[block, *whole, block] + [smem] * with_loss,
        out_specs=(block, smem) if with_loss else block,
        input_output_aliases={1 + count: 0},
        compiler_params=params(),
        cost_estimate=pl.CostEstimate(
            flops=4 * half * half * width, bytes_accessed=12 * half * width, transcendentals=0
        ),
        name="image_term" if with_loss else "text_term",
    )(mine, *[other for other, _ in others], total, *([loss] if with_loss else []))


def to_partner(part, mask):
    both = ("dx", "dy")
    count = lax.axis_size("dx") * lax.axis_size("dy")
    return lax.ppermute(part, both, [(k, k ^ mask) for k in range(count)])


def rounds(bits, scale, img, txt, both, match):
    half = img.shape[0]
    order = sorted(bits, key=lambda bit: -LOAD[bit])
    near = far = None
    for pair in RELAYED:
        if set(pair) <= set(bits) and LOAD[order[0]] < 2 * max(LOAD[bit] for bit in pair):
            near, far = sorted(pair, key=lambda bit: LOAD[bit])
    arrived = {}

    def send(bit, name, parts, mask=None):
        arrived[bit, name] = [(to_partner(p, mask or 1 << bit), None) for p in parts]

    def send_both(bit):
        sent = to_partner(both, 1 << bit)
        arrived[bit, "txt"], arrived[bit, "img"] = [(sent, 0)], [(sent, 1)]

    def cut(part):
        rows = 2 * half // PIECES
        return [part[at : at + rows] for at in range(0, half, rows)]

    image_grad, text_grad, loss = own_call(scale, img, txt, match)
    if near is not None:
        middle = [bit for bit in order if bit not in (near, far)]
        send(near, "txt", cut(txt))
        send(near, "img", cut(img))
        for name in ("txt", "img"):
            send(far, name, [p for p, _ in arrived[near, name]], 1 << near | 1 << far)
        for bit in middle:
            send_both(bit)
        steps = [(near, "txt"), (near, "img")]
        steps += [(bit, name) for bit in middle for name in ("txt", "img")]
        steps += [(far, "txt")]
        final = [far]
    else:
        heavy = [bit for bit in order if LOAD[bit] * 3 > LOAD[order[0]]]
        light = [bit for bit in order if bit not in heavy]
        for bit in heavy:
            send(bit, "txt", [txt])
            send(bit, "img", [img])
        for bit in light:
            send_both(bit)
        steps = [(bit, "txt") for bit in heavy]
        steps += [(bit, name) for bit in light for name in ("txt", "img")]
        final = heavy
    for bit, name in steps:
        image_grad, text_grad, loss = lax.optimization_barrier((image_grad, text_grad, loss))
        if name == "txt":
            image_grad, loss = add_call(scale, img, arrived[bit, "txt"], image_grad, loss)
        else:
            text_grad = add_call(scale, txt, arrived[bit, "img"], text_grad)
    image_grad, text_grad, loss = lax.optimization_barrier((image_grad, text_grad, loss))
    text_grad = add_call(scale, txt, sum((arrived[bit, "img"] for bit in final), []), text_grad)
    return image_grad, text_grad, loss


def body(low_count, all_bits, images, texts, match, masks):
    low_bits = low_count.bit_length() - 1
    half = images.shape[0]
    scale = 1.0 / (half * half * (masks.shape[0] + 1.0))
    img, txt, both, index = prepare_call(all_bits, masks, images, texts)
    sets = [
        (low, high, SECOND) for low in range(low_bits) for high in range(low + 1, all_bits - 1)
    ]
    branches = [partial(rounds, bits, scale) for bits in sets]
    return lax.switch(index[0], branches, img, txt, both, match)


def solution(mesh):
    rows = P(("dx", "dy"), None)
    low_count = mesh.shape["dy"]
    all_bits = (low_count * mesh.shape["dx"]).bit_length() - 1
    return jax.shard_map(
        partial(body, low_count, all_bits),
        mesh=mesh,
        in_specs=(rows, rows, rows, P()),
        out_specs=(rows, rows, P(("dx", "dy"))),
        check_vma=False,
    )
```

```python
from functools import partial

import jax
import jax.numpy as jnp
from jax import lax
from jax.experimental import pallas as pl
from jax.experimental.pallas import tpu as pltpu
from jax.sharding import PartitionSpec as P

MESH = pl.DeviceIdType.MESH
BIAS = -2.0
SECOND = 8
WIDE = 384
ROWS = 64
PIECE = 32

LOAD = {0: 0.2, 1: 1, 2: 1.01, 3: 4, 4: 4.01, 5: 1, 6: 2, 7: 1, 8: 1.02}
RELAYED = {(1, 2), (3, 4), (4, 5), (4, 6), (7, 8)}


def plan_for(bits):
    order = sorted(bits, key=lambda bit: LOAD[bit])
    for pair in RELAYED:
        if set(pair) <= set(bits) and LOAD[order[-1]] < 2 * max(LOAD[bit] for bit in pair):
            near, far = sorted(pair, key=lambda bit: LOAD[bit])
            (other,) = set(bits) - set(pair)
            return near, far, [(bit, half) for bit in (near, other, far) for half in (0, 1)]
    light = [bit for bit in order if LOAD[bit] * 3 <= LOAD[order[-1]]]
    heavy = [bit for bit in order if bit not in light]
    places = [(bit, half) for bit in light for half in (0, 1)]
    return None, None, places + [(bit, half) for half in (0, 1) for bit in heavy]


def flipped(index, mask):
    for k in range(16):
        if mask >> k & 1:
            step = 1 << k
            index = index + step * (1 - 2 * ((index // step) % 2))
    return index


def meet(bits, scale, low_count, *refs):
    (images_ref, texts_ref, match_ref, image_ref, text_ref, loss_ref, *refs) = refs
    (wide, blocks, grads, labels, logits, g, losses, *refs) = refs
    (load_sem, send_sem, recv_sem, near_sem, store_sem) = refs
    near, far, places = plan_for(bits)
    half_rows, width = texts_ref.shape
    pieces = half_rows // PIECE
    dx, dy = lax.axis_index("dx"), lax.axis_index("dy")

    def device(mask):
        return (flipped(dx, mask // low_count), flipped(dy, mask % low_count))

    at = {place: 2 + k for k, place in enumerate(places)}
    masks = {bit: 1 << bit for bit in bits}
    if far is not None:
        masks[far] = 1 << near | 1 << far

    def half_copy(bit, half):
        return pltpu.make_async_remote_copy(
            src_ref=blocks.at[half],
            dst_ref=blocks.at[at[bit, half]],
            send_sem=send_sem.at[at[bit, half]],
            recv_sem=recv_sem.at[at[bit, half]],
            device_id=device(masks[bit]),
            device_id_type=MESH,
        )

    def piece_copy(half, piece, forward):
        rows = pl.ds(pl.multiple_of(piece * PIECE, PIECE), PIECE)
        here, there = (at[near, 0] + half, at[far, 0] + half) if forward else (half, at[near, 0] + half)
        return pltpu.make_async_remote_copy(
            src_ref=blocks.at[here, rows],
            dst_ref=blocks.at[there, rows],
            send_sem=send_sem.at[there],
            recv_sem=recv_sem.at[there] if forward else near_sem.at[half, piece],
            device_id=device(masks[far if forward else near]),
            device_id_type=MESH,
        )

    loads = [
        pltpu.make_async_copy(ref, wide.at[half], load_sem.at[half])
        for half, ref in enumerate((texts_ref, images_ref))
    ]
    for load in loads:
        load.start()
    barrier = pltpu.get_barrier_semaphore()
    for bit in bits:
        pl.semaphore_signal(barrier, inc=1, device_id=device(masks[bit]), device_id_type=MESH)
    for half in (0, 1):
        loads[half].wait()

        @pl.loop(0, half_rows // ROWS)
        def _(step, half=half):
            rows = pl.ds(pl.multiple_of(step * ROWS, ROWS), ROWS)
            blocks[half, rows, :] = wide[half, rows, :].astype(jnp.bfloat16)

        if half == 0:
            pl.semaphore_wait(barrier, len(bits))
        if near is not None:

            @pl.loop(0, pieces)
            def _(piece, half=half):
                piece_copy(half, piece, False).start()

        for bit in sorted(bits, key=lambda bit: -LOAD[bit]):
            if bit not in (near, far):
                half_copy(bit, half).start()

    @pl.loop(0, half_rows // ROWS)
    def _(step):
        rows = pl.ds(pl.multiple_of(step * ROWS, ROWS), ROWS)
        zero = jnp.zeros((ROWS, width), jnp.float32)
        grads[0, rows, :] = zero
        grads[1, rows, :] = zero

    square = (half_rows, half_rows)
    row = lax.broadcasted_iota(jnp.int32, square, 0)
    column = lax.broadcasted_iota(jnp.int32, square, 1)
    short = jnp.bfloat16
    hits = jnp.where(row == match_ref[...], 1.0, 0.0).astype(short)
    labels[1] = hits
    labels[0] = across(jnp.where(row == column, 1.0, 0.0).astype(short), hits).astype(short)
    labels[2] = jnp.zeros(square, short)
    losses[...] = jnp.zeros_like(losses)

    ready = 2 if near is None else 4
    last_text = max(k for (_, half), k in at.items() if half == 0)
    store_image = pltpu.make_async_copy(grads.at[0], image_ref, store_sem.at[0])
    store_text = pltpu.make_async_copy(grads.at[1], text_ref, store_sem.at[1])

    @pl.loop(0, 2 + len(places))
    def _(k):
        side = (k == 1).astype(jnp.int32)
        for (_, half), place in at.items():
            if half == 1:
                side += (k == place).astype(jnp.int32)

        if near is not None:

            @pl.when(k == 2)
            def _():
                for half in (0, 1):

                    @pl.loop(0, pieces)
                    def _(piece, half=half):
                        piece_copy(half, piece, False).wait_recv()
                        piece_copy(half, piece, True).start()

        @pl.when(k >= ready)
        def _():
            pltpu.make_async_copy(blocks.at[k], blocks.at[k], recv_sem.at[k]).wait()

        logits[...] = jnp.full(square, BIAS, jnp.float32)

        @pl.loop(0, width // WIDE)
        def _(step):
            columns = pl.ds(pl.multiple_of(step * WIDE, WIDE), WIDE)
            logits[...] += across(blocks[1 - side, :, columns], blocks[k, :, columns])

        @pl.loop(0, half_rows // ROWS)
        def _(step):
            rows = pl.ds(pl.multiple_of(step * ROWS, ROWS), ROWS)
            x = logits[rows, :]
            label = labels[jnp.minimum(k, 2), rows, :].astype(jnp.float32)
            e = jnp.exp(-jnp.abs(x))
            s = jnp.where(x >= 0, 1.0, e) / (1.0 + e)
            g[rows, :] = (s - label).astype(short)
            loss = jnp.maximum(jnp.where(label > 0, -x, x), 0.0) + jnp.log1p(e)
            loss = jnp.sum(loss.reshape(ROWS // 8, 8, half_rows), axis=0)
            losses[...] += jnp.where(side == 0, loss, 0.0)

        @pl.loop(0, width // WIDE)
        def _(step):
            columns = pl.ds(pl.multiple_of(step * WIDE, WIDE), WIDE)
            grads[side, :, columns] += times(g[...], blocks[k, :, columns])

        @pl.when(k == last_text)
        def _():
            store_image.start()

    store_text.start()
    loss_ref[0] = jnp.sum(losses[...]) * scale
    for bit in bits:
        for half in (0, 1):
            half_copy(bit, half).wait_send()
    store_image.wait()
    store_text.wait()


def meet_call(bits, number, scale, low_count, images, texts, match):
    half, width = images.shape
    places = 2 + 2 * len(bits)
    grad = jax.ShapeDtypeStruct((half, width), jnp.float32)
    vmem = pl.BlockSpec(memory_space=pltpu.VMEM)
    anywhere = pl.BlockSpec(memory_space=pl.ANY)
    return pl.pallas_call(
        partial(meet, bits, scale, low_count),
        out_shape=(grad, grad, jax.ShapeDtypeStruct((1,), jnp.float32)),
        in_specs=[anywhere, anywhere, vmem],
        out_specs=(anywhere, anywhere, pl.BlockSpec(memory_space=pltpu.SMEM)),
        scratch_shapes=[
            pltpu.VMEM((2, half, width), jnp.float32),
            pltpu.VMEM((places, half, width), jnp.bfloat16),
            pltpu.VMEM((2, half, width), jnp.float32),
            pltpu.VMEM((3, half, half), jnp.bfloat16),
            pltpu.VMEM((half, half), jnp.float32),
            pltpu.VMEM((half, half), jnp.bfloat16),
            pltpu.VMEM((8, half), jnp.float32),
            pltpu.SemaphoreType.DMA((2,)),
            pltpu.SemaphoreType.DMA((places,)),
            pltpu.SemaphoreType.DMA((places,)),
            pltpu.SemaphoreType.DMA((2, half // PIECE)),
            pltpu.SemaphoreType.DMA((2,)),
        ],
        compiler_params=pltpu.CompilerParams(
            collective_id=number, has_side_effects=True, vmem_limit_bytes=24 * 2**20
        ),
        cost_estimate=pl.CostEstimate(
            flops=32 * half * half * width, bytes_accessed=16 * half * width, transcendentals=0
        ),
        name="meet_" + "_".join(str(bit) for bit in bits),
    )(images, texts, match)


def across(a, b):
    return lax.dot_general(a, b, (((1,), (1,)), ((), ())), preferred_element_type=jnp.float32)


def times(a, b):
    return jnp.dot(a, b, preferred_element_type=jnp.float32)


def choose(all_bits, masks_ref, index_ref):
    first, third = masks_ref[0], masks_ref[2]
    low, high = jnp.minimum(first, third), jnp.maximum(first, third)
    low_bit, high_bit = jnp.int32(0), jnp.int32(0)
    for k in range(1, all_bits):
        low_bit += (low >= 1 << k).astype(jnp.int32)
        high_bit += (high >= 1 << k).astype(jnp.int32)
    before = low_bit * (all_bits - 1) - low_bit * (low_bit + 1) // 2
    index_ref[0] = before + high_bit - low_bit - 1


def body(low_count, all_bits, images, texts, match, masks):
    low_bits = low_count.bit_length() - 1
    half = images.shape[0]
    scale = 1.0 / (half * half * (masks.shape[0] + 1.0))
    smem = pl.BlockSpec(memory_space=pltpu.SMEM)
    index = pl.pallas_call(
        partial(choose, all_bits),
        out_shape=jax.ShapeDtypeStruct((1,), jnp.int32),
        in_specs=[smem],
        out_specs=smem,
        name="choose",
    )(masks)
    sets = [
        (low, high, SECOND) for low in range(low_bits) for high in range(low + 1, all_bits - 1)
    ]
    branches = [
        partial(meet_call, bits, number, scale, low_count) for number, bits in enumerate(sets)
    ]
    return lax.switch(index[0], branches, images, texts, match)


def solution(mesh):
    rows = P(("dx", "dy"), None)
    low_count = mesh.shape["dy"]
    all_bits = (low_count * mesh.shape["dx"]).bit_length() - 1
    return jax.shard_map(
        partial(body, low_count, all_bits),
        mesh=mesh,
        in_specs=(rows, rows, rows, P()),
        out_specs=(rows, rows, P(("dx", "dy"))),
        check_vma=False,
    )
```

```python
from functools import partial

import jax
import jax.numpy as jnp
from jax import lax
from jax.experimental import pallas as pl
from jax.experimental.pallas import tpu as pltpu
from jax.sharding import PartitionSpec as P

MESH = pl.DeviceIdType.MESH
BIAS = -2.0
SECOND = 8
WIDE = 384
ROWS = 64
PIECE = 32

LOAD = {0: 0.2, 1: 1, 2: 1.01, 3: 4, 4: 4.01, 5: 1, 6: 2, 7: 1, 8: 1.02}
RELAYED = {(1, 2), (3, 4), (4, 5), (4, 6), (7, 8)}


def plan_for(bits, half_rows):
    def whole(bit, half):
        return half, [(bit, 0, 0, half_rows)]

    order = sorted(bits, key=lambda bit: LOAD[bit])
    for pair in RELAYED:
        if set(pair) <= set(bits) and LOAD[order[-1]] < 2 * max(LOAD[bit] for bit in pair):
            near, far = sorted(pair, key=lambda bit: LOAD[bit])
            (other,) = set(bits) - set(pair)
            pieces = half_rows // PIECE
            if LOAD[other] * 2 < LOAD[far]:
                uses = [(other, 0), (other, 1), (near, 0), (far, 0), (near, 1), (far, 1)]
                passed = [0, 0, pieces // 4, pieces // 2, pieces, pieces * 3 // 2, 2 * pieces, 2 * pieces]
            else:
                uses = [(near, 0), (other, 0), (far, 0), (near, 1), (other, 1), (far, 1)]
                passed = [0, 0, pieces, pieces * 5 // 4, pieces * 3 // 2, 2 * pieces, 2 * pieces, 2 * pieces]
            return near, far, [whole(*use) for use in uses], passed
    light = [bit for bit in order if LOAD[bit] * 3 <= LOAD[order[-1]]]
    heavy = [bit for bit in order if bit not in light]
    tiles = [whole(bit, half) for bit in light for half in (0, 1)] + [whole(bit, 0) for bit in heavy]
    sent = dict.fromkeys(heavy, 0)
    for at in range(len(heavy)):
        parts, filled = [], 0
        for turn, bit in enumerate(heavy):
            rows = half_rows // len(heavy) // 16 * 16
            if turn == at:
                rows = half_rows - rows * (len(heavy) - 1)
            parts.append((bit, sent[bit], filled, rows))
            sent[bit] += rows
            filled += rows
        tiles.append((1, parts))
    return None, None, tiles, None


def flipped(index, mask):
    for k in range(16):
        if mask >> k & 1:
            step = 1 << k
            index = index + step * (1 - 2 * ((index // step) % 2))
    return index


def meet(bits, scale, low_count, *refs):
    (own_ref, match_ref, image_ref, text_ref, loss_ref, *refs) = refs
    (blocks, labels, logits, g, losses, own_sem, send_sem, recv_sem, near_sem) = refs
    _, half_rows, width = own_ref.shape
    near, far, tiles, passed = plan_for(bits, half_rows)
    pieces = half_rows // PIECE
    dx, dy = lax.axis_index("dx"), lax.axis_index("dy")

    def device(mask):
        return (flipped(dx, mask // low_count), flipped(dy, mask % low_count))

    masks = {bit: 1 << bit for bit in bits}
    if far is not None:
        masks[far] = 1 << near | 1 << far
    barrier = pltpu.get_barrier_semaphore()
    for bit in bits:
        pl.semaphore_signal(barrier, inc=1, device_id=device(masks[bit]), device_id_type=MESH)

    first_row = {(bit, half): 2 + k for k, (half, parts) in enumerate(tiles) for bit, *_ in parts}
    keep = pltpu.make_async_copy(own_ref, blocks.at[pl.ds(0, 2)], own_sem)
    keep.start()

    def part_copy(k, half, part):
        bit, start, row, rows = part
        return pltpu.make_async_remote_copy(
            src_ref=own_ref.at[half, pl.ds(start, rows)],
            dst_ref=blocks.at[k, pl.ds(row, rows)],
            send_sem=send_sem.at[k],
            recv_sem=recv_sem.at[k],
            device_id=device(masks[bit]),
            device_id_type=MESH,
        )

    def piece_copy(half, piece, forward):
        rows = pl.ds(pl.multiple_of(piece * PIECE, PIECE), PIECE)
        here = first_row[near, 0] + half * (first_row[near, 1] - first_row[near, 0])
        there = first_row[far, 0] + half * (first_row[far, 1] - first_row[far, 0])
        return pltpu.make_async_remote_copy(
            src_ref=blocks.at[here, rows] if forward else own_ref.at[half, rows],
            dst_ref=blocks.at[there if forward else here, rows],
            send_sem=send_sem.at[there if forward else here],
            recv_sem=recv_sem.at[there] if forward else near_sem.at[half, piece],
            device_id=device(masks[far if forward else near]),
            device_id_type=MESH,
        )

    pl.semaphore_wait(barrier, len(bits))
    sends = [
        (half, -LOAD[part[0]], part[1], k, part)
        for k, (half, parts) in enumerate(tiles, 2)
        for part in parts
        if part[0] not in (near, far)
    ]
    for half in (0, 1):
        if near is not None:

            @pl.loop(0, pieces)
            def _(piece, half=half):
                piece_copy(half, piece, False).start()

        for _, _, _, k, part in sorted(send for send in sends if send[0] == half):
            part_copy(k, half, part).start()

    @pl.loop(0, half_rows // ROWS)
    def _(step):
        rows = pl.ds(pl.multiple_of(step * ROWS, ROWS), ROWS)
        zero = jnp.zeros((ROWS, width), jnp.float32)
        image_ref[rows, :] = zero
        text_ref[rows, :] = zero

    square = (half_rows, half_rows)
    row = lax.broadcasted_iota(jnp.int32, square, 0)
    column = lax.broadcasted_iota(jnp.int32, square, 1)
    short = jnp.bfloat16
    hits = jnp.where(row == match_ref[...], 1.0, 0.0).astype(short)
    labels[1] = hits
    labels[0] = across(jnp.where(row == column, 1.0, 0.0).astype(short), hits).astype(short)
    labels[2] = jnp.zeros(square, short)
    losses[...] = jnp.zeros_like(losses)
    keep.wait()

    def chosen(k, numbers):
        return sum(((k == number).astype(jnp.int32) for number in numbers), jnp.int32(0))

    @pl.loop(0, 2 + len(tiles))
    def _(k):
        side = chosen(k, [1] + [at for at, (half, _) in enumerate(tiles, 2) if half == 1])

        if near is not None:
            low = sum((more - less) * (k > at).astype(jnp.int32) for at, (less, more) in enumerate(zip([0] + passed, passed)) if more > less)
            high = sum((more - less) * (k >= at).astype(jnp.int32) for at, (less, more) in enumerate(zip([0] + passed, passed)) if more > less)

            @pl.loop(low, high)
            def _(at):
                half = at // pieces
                piece = at - half * pieces
                piece_copy(half, piece, False).wait_recv()
                piece_copy(half, piece, True).start()

            waits = chosen(k, [at for at, (_, parts) in enumerate(tiles, 2) if parts[0][0] != near])
        else:
            waits = (k >= 2).astype(jnp.int32)

        @pl.when(waits == 1)
        def _():
            pltpu.make_async_copy(blocks.at[k], blocks.at[k], recv_sem.at[k]).wait()

        logits[...] = jnp.full(square, BIAS, jnp.float32)

        @pl.loop(0, width // WIDE)
        def _(step):
            columns = pl.ds(pl.multiple_of(step * WIDE, WIDE), WIDE)
            logits[...] += across(blocks[1 - side, :, columns], blocks[k, :, columns])

        @pl.loop(0, half_rows // ROWS)
        def _(step):
            rows = pl.ds(pl.multiple_of(step * ROWS, ROWS), ROWS)
            x = logits[rows, :]
            label = labels[jnp.minimum(k, 2), rows, :].astype(jnp.float32)
            e = jnp.exp(-jnp.abs(x))
            s = jnp.where(x >= 0, 1.0, e) / (1.0 + e)
            g[rows, :] = (s - label).astype(short)

        @pl.loop(0, (1 - side) * (half_rows // ROWS))
        def _(step):
            rows = pl.ds(pl.multiple_of(step * ROWS, ROWS), ROWS)
            x = logits[rows, :]
            label = labels[jnp.minimum(k, 2), rows, :].astype(jnp.float32)
            loss = jnp.maximum(jnp.where(label > 0, -x, x), 0.0) + jnp.log1p(jnp.exp(-jnp.abs(x)))
            losses[...] += jnp.sum(loss.reshape(ROWS // 8, 8, half_rows), axis=0)

        for number, grad_ref in enumerate((image_ref, text_ref)):

            @pl.loop(0, (side == number).astype(jnp.int32) * (width // WIDE))
            def _(step, grad_ref=grad_ref):
                columns = pl.ds(pl.multiple_of(step * WIDE, WIDE), WIDE)
                grad_ref[:, columns] += times(g[...], blocks[k, :, columns])

    loss_ref[0] = jnp.sum(losses[...]) * scale

    @pl.loop(2, 2 + len(tiles))
    def _(k):
        side = chosen(k, [at for at, (half, _) in enumerate(tiles, 2) if half == 1])
        pltpu.make_async_copy(own_ref.at[side], own_ref.at[side], send_sem.at[k]).wait()


def meet_call(bits, number, scale, low_count, own, match):
    _, half, width = own.shape
    places = 2 + 2 * len(bits)
    vmem = pl.BlockSpec(memory_space=pltpu.VMEM)
    return pl.pallas_call(
        partial(meet, bits, scale, low_count),
        out_shape=(
            pltpu.VMEM((half, width), jnp.float32),
            pltpu.VMEM((half, width), jnp.float32),
            jax.ShapeDtypeStruct((1,), jnp.float32),
        ),
        in_specs=[vmem, vmem],
        out_specs=(vmem, vmem, pl.BlockSpec(memory_space=pltpu.SMEM)),
        scratch_shapes=[
            pltpu.VMEM((places, half, width), jnp.bfloat16),
            pltpu.VMEM((3, half, half), jnp.bfloat16),
            pltpu.VMEM((half, half), jnp.float32),
            pltpu.VMEM((half, half), jnp.bfloat16),
            pltpu.VMEM((8, half), jnp.float32),
            pltpu.SemaphoreType.DMA,
            pltpu.SemaphoreType.DMA((places,)),
            pltpu.SemaphoreType.DMA((places,)),
            pltpu.SemaphoreType.DMA((2, half // PIECE)),
        ],
        compiler_params=pltpu.CompilerParams(
            collective_id=number, has_side_effects=True, vmem_limit_bytes=24 * 2**20
        ),
        cost_estimate=pl.CostEstimate(
            flops=32 * half * half * width, bytes_accessed=16 * half * width, transcendentals=0
        ),
        name="meet_" + "_".join(str(bit) for bit in bits),
    )(own, match)


def across(a, b):
    return lax.dot_general(a, b, (((1,), (1,)), ((), ())), preferred_element_type=jnp.float32)


def times(a, b):
    return jnp.dot(a, b, preferred_element_type=jnp.float32)


def prepare(all_bits, masks_ref, images_ref, texts_ref, own_ref, index_ref, wide, load_sem):
    half_rows = texts_ref.shape[0]
    loads = [
        (half, at, pltpu.make_async_copy(
            ref.at[pl.ds(at, ROWS)], wide.at[half, pl.ds(at, ROWS)], load_sem.at[half, at // ROWS]
        ))
        for half, ref in enumerate((texts_ref, images_ref))
        for at in range(0, half_rows, ROWS)
    ]
    for _, _, load in loads:
        load.start()
    first, third = masks_ref[0], masks_ref[2]
    low, high = jnp.minimum(first, third), jnp.maximum(first, third)
    low_bit, high_bit = jnp.int32(0), jnp.int32(0)
    for k in range(1, all_bits):
        low_bit += (low >= 1 << k).astype(jnp.int32)
        high_bit += (high >= 1 << k).astype(jnp.int32)
    before = low_bit * (all_bits - 1) - low_bit * (low_bit + 1) // 2
    index_ref[0] = before + high_bit - low_bit - 1
    for half, at, load in loads:
        load.wait()
        own_ref[half, pl.ds(at, ROWS), :] = wide[half, pl.ds(at, ROWS), :].astype(jnp.bfloat16)


def body(low_count, all_bits, images, texts, match, masks):
    low_bits = low_count.bit_length() - 1
    half, width = images.shape
    scale = 1.0 / (half * half * (masks.shape[0] + 1.0))
    smem = pl.BlockSpec(memory_space=pltpu.SMEM)
    anywhere = pl.BlockSpec(memory_space=pl.ANY)
    own, index = pl.pallas_call(
        partial(prepare, all_bits),
        out_shape=(pltpu.VMEM((2, half, width), jnp.bfloat16), pltpu.SMEM((1,), jnp.int32)),
        in_specs=[smem, anywhere, anywhere],
        out_specs=(pl.BlockSpec(memory_space=pltpu.VMEM), smem),
        scratch_shapes=[
            pltpu.VMEM((2, half, width), jnp.float32),
            pltpu.SemaphoreType.DMA((2, half // ROWS)),
        ],
        compiler_params=pltpu.CompilerParams(vmem_limit_bytes=16 * 2**20),
        name="prepare",
    )(*(pltpu.with_memory_space_constraint(x, pltpu.HBM) for x in (masks, images, texts)))
    sets = [
        (low, high, SECOND) for low in range(low_bits) for high in range(low + 1, all_bits - 1)
    ]
    branches = [
        partial(meet_call, bits, number, scale, low_count) for number, bits in enumerate(sets)
    ]
    return lax.switch(index[0], branches, own, match)


def solution(mesh):
    rows = P(("dx", "dy"), None)
    low_count = mesh.shape["dy"]
    all_bits = (low_count * mesh.shape["dx"]).bit_length() - 1
    return jax.shard_map(
        partial(body, low_count, all_bits),
        mesh=mesh,
        in_specs=(rows, rows, rows, P()),
        out_specs=(rows, rows, P(("dx", "dy"))),
        check_vma=False,
    )
```

```python
from functools import partial

import jax
import jax.numpy as jnp
from jax import lax
from jax.experimental import pallas as pl
from jax.experimental.pallas import tpu as pltpu
from jax.sharding import PartitionSpec as P

MESH = pl.DeviceIdType.MESH
BIAS = -2.0
SECOND = 8
WIDE = 384
ROWS = 64
PIECE = 32
STORES = 4

LOAD = {0: 0.2, 1: 1, 2: 1.01, 3: 4, 4: 4.01, 5: 1, 6: 2, 7: 1, 8: 1.02}
RELAYED = {(1, 2), (3, 4), (4, 5), (4, 6), (7, 8)}


def plan_for(bits, half_rows):
    def whole(bit, half):
        return half, [(bit, 0, 0, half_rows)]

    order = sorted(bits, key=lambda bit: LOAD[bit])
    for pair in RELAYED:
        if set(pair) <= set(bits) and LOAD[order[-1]] < 2 * max(LOAD[bit] for bit in pair):
            near, far = sorted(pair, key=lambda bit: LOAD[bit])
            (other,) = set(bits) - set(pair)
            pieces = half_rows // PIECE
            if LOAD[other] * 2 < LOAD[far]:
                uses = [(other, 0), (other, 1), (near, 0), (far, 0), (near, 1), (far, 1)]
                passed = [0, 0, pieces // 4, pieces // 2, pieces, pieces * 3 // 2, 2 * pieces, 2 * pieces]
            else:
                uses = [(near, 0), (other, 0), (far, 0), (near, 1), (other, 1), (far, 1)]
                passed = [0, 0, pieces, pieces * 5 // 4, pieces * 3 // 2, 2 * pieces, 2 * pieces, 2 * pieces]
            return near, far, [whole(*use) for use in uses], passed
    light = [bit for bit in order if LOAD[bit] * 3 <= LOAD[order[-1]]]
    heavy = [bit for bit in order if bit not in light]
    tiles = [whole(bit, half) for bit in light for half in (0, 1)] + [whole(bit, 0) for bit in heavy]
    sent = dict.fromkeys(heavy, 0)
    for at in range(len(heavy)):
        parts, filled = [], 0
        for turn, bit in enumerate(heavy):
            rows = half_rows // len(heavy) // 16 * 16
            if turn == at:
                rows = half_rows - rows * (len(heavy) - 1)
            parts.append((bit, sent[bit], filled, rows))
            sent[bit] += rows
            filled += rows
        tiles.append((1, parts))
    return None, None, tiles, None


def flipped(index, mask):
    for k in range(16):
        if mask >> k & 1:
            step = 1 << k
            index = index + step * (1 - 2 * ((index // step) % 2))
    return index


def meet(bits, scale, low_count, *refs):
    (own_ref, images_ref, match_ref, image_ref, text_ref, blocks, g, loss_ref, *refs) = refs
    (wide, labels, logits, losses, own_sem, load_sem, send_sem, recv_sem, near_sem) = refs
    half_rows, width = own_ref.shape
    near, far, tiles, passed = plan_for(bits, half_rows)
    pieces = half_rows // PIECE
    dx, dy = lax.axis_index("dx"), lax.axis_index("dy")

    def device(mask):
        return (flipped(dx, mask // low_count), flipped(dy, mask % low_count))

    masks = {bit: 1 << bit for bit in bits}
    if far is not None:
        masks[far] = 1 << near | 1 << far
    barrier = pltpu.get_barrier_semaphore()
    for bit in bits:
        pl.semaphore_signal(barrier, inc=1, device_id=device(masks[bit]), device_id_type=MESH)

    first_row = {(bit, half): 2 + k for k, (half, parts) in enumerate(tiles) for bit, *_ in parts}
    keep = pltpu.make_async_copy(own_ref, blocks.at[0], own_sem)
    keep.start()
    sources = (own_ref, blocks.at[1])

    def load(step):
        rows = pl.ds(pl.multiple_of(step * ROWS, ROWS), ROWS)
        return rows, pltpu.make_async_copy(images_ref.at[rows], wide.at[rows], load_sem.at[step])

    steps = half_rows // ROWS
    for step in range(steps):
        load(step)[1].start()

    def part_copy(k, half, part):
        bit, start, row, rows = part
        return pltpu.make_async_remote_copy(
            src_ref=sources[half].at[pl.ds(start, rows)],
            dst_ref=blocks.at[k, pl.ds(row, rows)],
            send_sem=send_sem.at[k],
            recv_sem=recv_sem.at[k],
            device_id=device(masks[bit]),
            device_id_type=MESH,
        )

    def piece_copy(half, piece, forward):
        rows = pl.ds(pl.multiple_of(piece * PIECE, PIECE), PIECE)
        here = first_row[near, 0] + half * (first_row[near, 1] - first_row[near, 0])
        source = blocks.at[here] if forward else sources[half] if isinstance(half, int) else own_ref
        there = first_row[far, 0] + half * (first_row[far, 1] - first_row[far, 0])
        return pltpu.make_async_remote_copy(
            src_ref=source.at[rows],
            dst_ref=blocks.at[there if forward else here, rows],
            send_sem=send_sem.at[there if forward else here],
            recv_sem=recv_sem.at[there] if forward else near_sem.at[half, piece],
            device_id=device(masks[far if forward else near]),
            device_id_type=MESH,
        )

    pl.semaphore_wait(barrier, len(bits))
    sends = [
        (half, -LOAD[part[0]], part[1], k, part)
        for k, (half, parts) in enumerate(tiles, 2)
        for part in parts
        if part[0] not in (near, far)
    ]
    for half in (0, 1):
        if half == 1:

            @pl.loop(0, steps)
            def _(step):
                rows, arriving = load(step)
                arriving.wait()
                blocks[1, rows, :] = wide[rows, :].astype(jnp.bfloat16)

        if near is not None:

            @pl.loop(0, pieces)
            def _(piece, half=half):
                piece_copy(half, piece, False).start()

        for _, _, _, k, part in sorted(send for send in sends if send[0] == half):
            part_copy(k, half, part).start()

    @pl.loop(0, steps)
    def _(step):
        rows = pl.ds(pl.multiple_of(step * ROWS, ROWS), ROWS)
        zero = jnp.zeros((ROWS, width), jnp.float32)
        image_ref[rows, :] = zero
        text_ref[rows, :] = zero

    square = (half_rows, half_rows)
    row = lax.broadcasted_iota(jnp.int32, square, 0)
    column = lax.broadcasted_iota(jnp.int32, square, 1)
    short = jnp.bfloat16
    hits = jnp.where(row == match_ref[...], 1.0, 0.0).astype(short)
    labels[1] = hits
    labels[0] = across(jnp.where(row == column, 1.0, 0.0).astype(short), hits).astype(short)
    labels[2] = jnp.zeros(square, short)
    losses[...] = jnp.zeros_like(losses)
    keep.wait()

    def chosen(k, numbers):
        return sum(((k == number).astype(jnp.int32) for number in numbers), jnp.int32(0))

    @pl.loop(0, 2 + len(tiles))
    def _(k):
        side = chosen(k, [1] + [at for at, (half, _) in enumerate(tiles, 2) if half == 1])

        if near is not None:
            low = sum((more - less) * (k > at).astype(jnp.int32) for at, (less, more) in enumerate(zip([0] + passed, passed)) if more > less)
            high = sum((more - less) * (k >= at).astype(jnp.int32) for at, (less, more) in enumerate(zip([0] + passed, passed)) if more > less)

            @pl.loop(low, high)
            def _(at):
                half = at // pieces
                piece = at - half * pieces
                piece_copy(half, piece, False).wait_recv()
                piece_copy(half, piece, True).start()

            waits = chosen(k, [at for at, (_, parts) in enumerate(tiles, 2) if parts[0][0] != near])
        else:
            waits = (k >= 2).astype(jnp.int32)

        logits[...] = jnp.full(square, BIAS, jnp.float32)

        @pl.when(k > len(tiles))
        def _():
            loss_ref[0] = jnp.sum(losses[...]) * scale

        @pl.when(waits == 1)
        def _():
            pltpu.make_async_copy(blocks.at[k], blocks.at[k], recv_sem.at[k]).wait()

        @pl.loop(0, width // WIDE)
        def _(step):
            columns = pl.ds(pl.multiple_of(step * WIDE, WIDE), WIDE)
            logits[...] += across(blocks[1 - side, :, columns], blocks[k, :, columns])

        @pl.loop(0, half_rows // ROWS)
        def _(step):
            rows = pl.ds(pl.multiple_of(step * ROWS, ROWS), ROWS)
            x = logits[rows, :]
            label = labels[jnp.minimum(k, 2), rows, :].astype(jnp.float32)
            e = jnp.exp(-jnp.abs(x))
            s = jnp.where(x >= 0, 1.0, e) / (1.0 + e)
            g[rows, :] = (s - label).astype(short)

        @pl.loop(0, (1 - side) * (half_rows // ROWS))
        def _(step):
            rows = pl.ds(pl.multiple_of(step * ROWS, ROWS), ROWS)
            x = logits[rows, :]
            label = labels[jnp.minimum(k, 2), rows, :].astype(jnp.float32)
            loss = jnp.maximum(jnp.where(label > 0, -x, x), 0.0) + jnp.log1p(jnp.exp(-jnp.abs(x)))
            losses[...] += jnp.sum(loss.reshape(ROWS // 8, 8, half_rows), axis=0)

        for number, grad_ref in enumerate((image_ref, text_ref)):
            now = jnp.logical_and(side == number, k <= len(tiles)).astype(jnp.int32)

            @pl.loop(0, now * (width // WIDE))
            def _(step, grad_ref=grad_ref):
                columns = pl.ds(pl.multiple_of(step * WIDE, WIDE), WIDE)
                grad_ref[:, columns] += times(g[...], blocks[k, :, columns])

    @pl.loop(2, 2 + len(tiles))
    def _(k):
        pltpu.make_async_copy(own_ref, own_ref, send_sem.at[k]).wait()


def meet_call(bits, number, scale, low_count, own, images, match):
    half, width = own.shape
    places = 2 + 2 * len(bits)
    vmem = pl.BlockSpec(memory_space=pltpu.VMEM)
    return pl.pallas_call(
        partial(meet, bits, scale, low_count),
        out_shape=(
            pltpu.VMEM((half, width), jnp.float32),
            pltpu.VMEM((half, width), jnp.float32),
            pltpu.VMEM((places, half, width), jnp.bfloat16),
            pltpu.VMEM((half, half), jnp.bfloat16),
            jax.ShapeDtypeStruct((1,), jnp.float32),
        ),
        in_specs=[vmem, pl.BlockSpec(memory_space=pl.ANY), vmem],
        out_specs=(vmem, vmem, vmem, vmem, pl.BlockSpec(memory_space=pltpu.SMEM)),
        scratch_shapes=[
            pltpu.VMEM((half, width), jnp.float32),
            pltpu.VMEM((3, half, half), jnp.bfloat16),
            pltpu.VMEM((half, half), jnp.float32),
            pltpu.VMEM((8, half), jnp.float32),
            pltpu.SemaphoreType.DMA,
            pltpu.SemaphoreType.DMA((half // ROWS,)),
            pltpu.SemaphoreType.DMA((places,)),
            pltpu.SemaphoreType.DMA((places,)),
            pltpu.SemaphoreType.DMA((2, half // PIECE)),
        ],
        compiler_params=pltpu.CompilerParams(
            collective_id=number, has_side_effects=True, vmem_limit_bytes=24 * 2**20
        ),
        cost_estimate=pl.CostEstimate(
            flops=32 * half * half * width, bytes_accessed=16 * half * width, transcendentals=0
        ),
        name="meet_" + "_".join(str(bit) for bit in bits),
    )(own, images, match)


def finish(image_ref, text_ref, blocks, g, image_out, text_out, ready, store_sem):
    half_rows, width = image_ref.shape
    rows = half_rows // STORES
    stores = [
        pltpu.make_async_copy(
            image_ref.at[pl.ds(at * rows, rows)], image_out.at[pl.ds(at * rows, rows)], store_sem.at[at]
        )
        for at in range(STORES)
    ]
    for store in stores:
        store.start()
    for at in range(width // WIDE):
        columns = pl.ds(at * WIDE, WIDE)
        ready[:, columns] = text_ref[:, columns] + times(g[...], blocks[blocks.shape[0] - 1, :, columns])
        store = pltpu.make_async_copy(
            ready.at[:, columns], text_out.at[:, columns], store_sem.at[STORES + at]
        )
        store.start()
        stores.append(store)
    for store in stores:
        store.wait()


def finish_call(image, text, blocks, g):
    half, width = image.shape
    grad = jax.ShapeDtypeStruct((half, width), jnp.float32)
    vmem = pl.BlockSpec(memory_space=pltpu.VMEM)
    anywhere = pl.BlockSpec(memory_space=pl.ANY)
    return pl.pallas_call(
        finish,
        out_shape=(grad, grad),
        in_specs=[anywhere, vmem, vmem, vmem],
        out_specs=(anywhere, anywhere),
        scratch_shapes=[
            pltpu.VMEM((half, width), jnp.float32),
            pltpu.SemaphoreType.DMA((STORES + width // WIDE,)),
        ],
        compiler_params=pltpu.CompilerParams(vmem_limit_bytes=16 * 2**20),
        name="finish",
    )(image, text, blocks, g)


def across(a, b):
    return lax.dot_general(a, b, (((1,), (1,)), ((), ())), preferred_element_type=jnp.float32)


def times(a, b):
    return jnp.dot(a, b, preferred_element_type=jnp.float32)


def prepare(all_bits, masks_ref, texts_ref, own_ref, index_ref, wide, load_sem):
    loads = [
        pltpu.make_async_copy(
            texts_ref.at[pl.ds(at, ROWS)], wide.at[pl.ds(at, ROWS)], load_sem.at[at // ROWS]
        )
        for at in range(0, texts_ref.shape[0], ROWS)
    ]
    for load in loads:
        load.start()
    first, third = masks_ref[0], masks_ref[2]
    low, high = jnp.minimum(first, third), jnp.maximum(first, third)
    low_bit, high_bit = jnp.int32(0), jnp.int32(0)
    for k in range(1, all_bits):
        low_bit += (low >= 1 << k).astype(jnp.int32)
        high_bit += (high >= 1 << k).astype(jnp.int32)
    before = low_bit * (all_bits - 1) - low_bit * (low_bit + 1) // 2
    index_ref[0] = before + high_bit - low_bit - 1
    for at, load in enumerate(loads):
        load.wait()
        rows = pl.ds(at * ROWS, ROWS)
        own_ref[rows, :] = wide[rows, :].astype(jnp.bfloat16)


def body(low_count, all_bits, images, texts, match, masks):
    low_bits = low_count.bit_length() - 1
    half, width = images.shape
    scale = 1.0 / (half * half * (masks.shape[0] + 1.0))
    images, texts, masks = (
        pltpu.with_memory_space_constraint(x, pltpu.HBM) for x in (images, texts, masks)
    )
    smem = pl.BlockSpec(memory_space=pltpu.SMEM)
    own, index = pl.pallas_call(
        partial(prepare, all_bits),
        out_shape=(pltpu.VMEM((half, width), jnp.bfloat16), pltpu.SMEM((1,), jnp.int32)),
        in_specs=[smem, pl.BlockSpec(memory_space=pl.ANY)],
        out_specs=(pl.BlockSpec(memory_space=pltpu.VMEM), smem),
        scratch_shapes=[
            pltpu.VMEM((half, width), jnp.float32),
            pltpu.SemaphoreType.DMA((half // ROWS,)),
        ],
        compiler_params=pltpu.CompilerParams(vmem_limit_bytes=16 * 2**20),
        name="prepare",
    )(masks, texts)
    sets = [
        (low, high, SECOND) for low in range(low_bits) for high in range(low + 1, all_bits - 1)
    ]
    branches = [
        partial(meet_call, bits, number, scale, low_count) for number, bits in enumerate(sets)
    ]
    *terms, loss = lax.switch(index[0], branches, own, images, match)
    return (*finish_call(*terms), loss)


def solution(mesh):
    rows = P(("dx", "dy"), None)
    low_count = mesh.shape["dy"]
    all_bits = (low_count * mesh.shape["dx"]).bit_length() - 1
    return jax.shard_map(
        partial(body, low_count, all_bits),
        mesh=mesh,
        in_specs=(rows, rows, rows, P()),
        out_specs=(rows, rows, P(("dx", "dy"))),
        check_vma=False,
    )
```

```python
from functools import partial

import jax
import jax.numpy as jnp
from jax import lax
from jax.experimental import pallas as pl
from jax.experimental.pallas import tpu as pltpu
from jax.sharding import PartitionSpec as P

MESH = pl.DeviceIdType.MESH
BIAS = -2.0
SECOND = 8
WIDE = 384
ROWS = 64
PIECE = 32

LOAD = {0: 0.2, 1: 1, 2: 1.01, 3: 4, 4: 4.01, 5: 1, 6: 2, 7: 1, 8: 1.02}
HALFWAY, NEIGHBOUR = 4, 5
RELAYED = {(1, 2), (3, 4), (4, 5), (4, 6), (7, 8)}


def plan_for(bits, half_rows):
    def whole(bit, half):
        return half, [(bit, 0, 0, half_rows)]

    order = sorted(bits, key=lambda bit: LOAD[bit])
    pieces = half_rows // PIECE
    for pair in RELAYED:
        if set(pair) <= set(bits) and LOAD[order[-1]] < 2 * max(LOAD[bit] for bit in pair):
            near, far = sorted(pair, key=lambda bit: LOAD[bit])
            (other,) = set(bits) - set(pair)
            if LOAD[other] * 2 < LOAD[far]:
                uses = [(other, 0), (near, 0), (other, 1), (far, 0), (near, 1), (far, 1)]
                passed = [1, 2, 4, pieces, pieces + 4, pieces + 6, 2 * pieces, 2 * pieces]
            else:
                uses = [(near, 0), (other, 0), (far, 0), (near, 1), (other, 1), (far, 1)]
                passed = [1, 2, pieces, pieces + 2, pieces + 4, 2 * pieces, 2 * pieces, 2 * pieces]
            return near, far, [whole(*use) for use in uses], passed
    if order[-1] == HALFWAY:
        uses = [(bit, half) for part in (order[:-1], order[-1:]) for half in (0, 1) for bit in part]
        passed = [1, 2, 6, pieces, pieces + 4, pieces + 6, 2 * pieces, 2 * pieces]
        return NEIGHBOUR, HALFWAY, [whole(*use) for use in uses], passed
    light = [bit for bit in order if LOAD[bit] * 3 <= LOAD[order[-1]]]
    heavy = [bit for bit in order if bit not in light]
    tiles = [whole(bit, half) for bit in light for half in (0, 1)] + [whole(bit, 0) for bit in heavy]
    sent = dict.fromkeys(heavy, 0)
    for at in range(len(heavy)):
        parts, filled = [], 0
        for turn, bit in enumerate(heavy):
            rows = half_rows // len(heavy) // 16 * 16
            if turn == at:
                rows = half_rows - rows * (len(heavy) - 1)
            parts.append((bit, sent[bit], filled, rows))
            sent[bit] += rows
            filled += rows
        tiles.append((1, parts))
    return None, None, tiles, None


def flipped(index, mask):
    for k in range(16):
        if mask >> k & 1:
            step = 1 << k
            index = index + step * (1 - 2 * ((index // step) % 2))
    return index


def meet(bits, scale, low_count, *refs):
    (own_ref, match_ref, image_ref, text_ref, loss_ref, *refs) = refs
    (blocks, relay, labels, logits, g, losses, own_sem, send_sem, recv_sem, relay_sem, near_sem) = refs
    _, half_rows, width = own_ref.shape
    near, far, tiles, passed = plan_for(bits, half_rows)
    pieces = half_rows // PIECE
    dx, dy = lax.axis_index("dx"), lax.axis_index("dy")

    def device(mask):
        return (flipped(dx, mask // low_count), flipped(dy, mask % low_count))

    masks = {bit: 1 << bit for bit in bits}
    if far is not None:
        masks[near] = 1 << near
        masks[far] = 1 << near | 1 << far
    barrier = pltpu.get_barrier_semaphore()
    for mask in masks.values():
        pl.semaphore_signal(barrier, inc=1, device_id=device(mask), device_id_type=MESH)

    first_row = {(bit, half): 2 + k for k, (half, parts) in enumerate(tiles) for bit, *_ in parts}
    keep = pltpu.make_async_copy(own_ref, blocks.at[pl.ds(0, 2)], own_sem)
    keep.start()

    def part_copy(k, half, part):
        bit, start, row, rows = part
        return pltpu.make_async_remote_copy(
            src_ref=own_ref.at[half, pl.ds(start, rows)],
            dst_ref=blocks.at[k, pl.ds(row, rows)],
            send_sem=send_sem.at[k],
            recv_sem=recv_sem.at[k],
            device_id=device(masks[bit]),
            device_id_type=MESH,
        )

    def piece_copy(half, piece, forward):
        rows = pl.ds(pl.multiple_of(piece * PIECE, PIECE), PIECE)
        there = first_row[far, 0] + half * (first_row[far, 1] - first_row[far, 0])
        if near in bits:
            here = first_row[near, 0] + half * (first_row[near, 1] - first_row[near, 0])
            stop, sent = blocks.at[here, rows], send_sem.at[here]
        else:
            stop, sent = relay.at[half, rows], relay_sem.at[half]
        return pltpu.make_async_remote_copy(
            src_ref=stop if forward else own_ref.at[half, rows],
            dst_ref=blocks.at[there, rows] if forward else stop,
            send_sem=send_sem.at[there] if forward else sent,
            recv_sem=recv_sem.at[there] if forward else near_sem.at[half, piece],
            device_id=device(masks[far if forward else near]),
            device_id_type=MESH,
        )

    pl.semaphore_wait(barrier, len(masks))
    sends = [
        (half, -LOAD[part[0]], part[1], k, part)
        for k, (half, parts) in enumerate(tiles, 2)
        for part in parts
        if part[0] not in (near, far)
    ]
    for half in (0, 1):
        if near is not None:

            @pl.loop(0, pieces)
            def _(piece, half=half):
                piece_copy(half, piece, False).start()

        for _, _, _, k, part in sorted(send for send in sends if send[0] == half):
            part_copy(k, half, part).start()

    @pl.loop(0, half_rows // ROWS)
    def _(step):
        rows = pl.ds(pl.multiple_of(step * ROWS, ROWS), ROWS)
        zero = jnp.zeros((ROWS, width), jnp.float32)
        image_ref[rows, :] = zero
        text_ref[rows, :] = zero

    square = (half_rows, half_rows)
    row = lax.broadcasted_iota(jnp.int32, square, 0)
    column = lax.broadcasted_iota(jnp.int32, square, 1)
    short = jnp.bfloat16
    hits = jnp.where(row == match_ref[...], 1.0, 0.0).astype(short)
    labels[1] = hits
    labels[0] = across(jnp.where(row == column, 1.0, 0.0).astype(short), hits).astype(short)
    labels[2] = jnp.zeros(square, short)
    losses[...] = jnp.zeros_like(losses)
    keep.wait()

    def chosen(k, numbers):
        return sum(((k == number).astype(jnp.int32) for number in numbers), jnp.int32(0))

    @pl.loop(0, 2 + len(tiles))
    def _(k):
        side = chosen(k, [1] + [at for at, (half, _) in enumerate(tiles, 2) if half == 1])

        if near is not None:
            low = sum((more - less) * (k > at).astype(jnp.int32) for at, (less, more) in enumerate(zip([0] + passed, passed)) if more > less)
            high = sum((more - less) * (k >= at).astype(jnp.int32) for at, (less, more) in enumerate(zip([0] + passed, passed)) if more > less)

            @pl.loop(low, high)
            def _(at):
                half = at // pieces
                piece = at - half * pieces
                piece_copy(half, piece, False).wait_recv()
                piece_copy(half, piece, True).start()

            waits = chosen(k, [at for at, (_, parts) in enumerate(tiles, 2) if parts[0][0] != near])
        else:
            waits = (k >= 2).astype(jnp.int32)

        logits[...] = jnp.full(square, BIAS, jnp.float32)

        @pl.when(k > len(tiles))
        def _():
            loss_ref[0] = jnp.sum(losses[...]) * scale

        @pl.when(waits == 1)
        def _():
            pltpu.make_async_copy(blocks.at[k], blocks.at[k], recv_sem.at[k]).wait()

        @pl.loop(0, width // WIDE)
        def _(step):
            columns = pl.ds(pl.multiple_of(step * WIDE, WIDE), WIDE)
            logits[...] += across(blocks[1 - side, :, columns], blocks[k, :, columns])

        @pl.loop(0, half_rows // ROWS)
        def _(step):
            rows = pl.ds(pl.multiple_of(step * ROWS, ROWS), ROWS)
            x = logits[rows, :]
            label = labels[jnp.minimum(k, 2), rows, :].astype(jnp.float32)
            e = jnp.exp(-jnp.abs(x))
            s = jnp.where(x >= 0, 1.0, e) / (1.0 + e)
            g[rows, :] = (s - label).astype(short)

        @pl.loop(0, (1 - side) * (half_rows // ROWS))
        def _(step):
            rows = pl.ds(pl.multiple_of(step * ROWS, ROWS), ROWS)
            x = logits[rows, :]
            label = labels[jnp.minimum(k, 2), rows, :].astype(jnp.float32)
            loss = jnp.maximum(jnp.where(label > 0, -x, x), 0.0) + jnp.log1p(jnp.exp(-jnp.abs(x)))
            losses[...] += jnp.sum(loss.reshape(ROWS // 8, 8, half_rows), axis=0)

        for number, grad_ref in enumerate((image_ref, text_ref)):

            @pl.loop(0, (side == number).astype(jnp.int32) * (width // WIDE))
            def _(step, grad_ref=grad_ref):
                columns = pl.ds(pl.multiple_of(step * WIDE, WIDE), WIDE)
                grad_ref[:, columns] += times(g[...], blocks[k, :, columns])

    @pl.loop(2, 2 + len(tiles))
    def _(k):
        pltpu.make_async_copy(own_ref.at[0], own_ref.at[0], send_sem.at[k]).wait()

    if near is not None and near not in bits:
        for half in (0, 1):
            pltpu.make_async_copy(own_ref.at[half], own_ref.at[half], relay_sem.at[half]).wait()


def meet_call(bits, number, scale, low_count, own, match):
    _, half, width = own.shape
    places = 2 + 2 * len(bits)
    vmem = pl.BlockSpec(memory_space=pltpu.VMEM)
    return pl.pallas_call(
        partial(meet, bits, scale, low_count),
        out_shape=(
            pltpu.VMEM((half, width), jnp.float32),
            pltpu.VMEM((half, width), jnp.float32),
            jax.ShapeDtypeStruct((1,), jnp.float32),
        ),
        in_specs=[vmem, vmem],
        out_specs=(vmem, vmem, pl.BlockSpec(memory_space=pltpu.SMEM)),
        scratch_shapes=[
            pltpu.VMEM((places, half, width), jnp.bfloat16),
            pltpu.VMEM((2, half, width), jnp.bfloat16),
            pltpu.VMEM((3, half, half), jnp.bfloat16),
            pltpu.VMEM((half, half), jnp.float32),
            pltpu.VMEM((half, half), jnp.bfloat16),
            pltpu.VMEM((8, half), jnp.float32),
            pltpu.SemaphoreType.DMA,
            pltpu.SemaphoreType.DMA((places,)),
            pltpu.SemaphoreType.DMA((places,)),
            pltpu.SemaphoreType.DMA((2,)),
            pltpu.SemaphoreType.DMA((2, half // PIECE)),
        ],
        compiler_params=pltpu.CompilerParams(
            collective_id=number, has_side_effects=True, vmem_limit_bytes=24 * 2**20
        ),
        cost_estimate=pl.CostEstimate(
            flops=32 * half * half * width, bytes_accessed=16 * half * width, transcendentals=0
        ),
        name="meet_" + "_".join(str(bit) for bit in bits),
    )(own, match)


def across(a, b):
    return lax.dot_general(a, b, (((1,), (1,)), ((), ())), preferred_element_type=jnp.float32)


def times(a, b):
    return jnp.dot(a, b, preferred_element_type=jnp.float32)


def prepare(all_bits, masks_ref, images_ref, texts_ref, own_ref, index_ref, wide, load_sem):
    half_rows = texts_ref.shape[0]
    loads = [
        (half, at, pltpu.make_async_copy(
            ref.at[pl.ds(at, ROWS)], wide.at[half, pl.ds(at, ROWS)], load_sem.at[half, at // ROWS]
        ))
        for half, ref in enumerate((texts_ref, images_ref))
        for at in range(0, half_rows, ROWS)
    ]
    for _, _, load in loads:
        load.start()
    first, third = masks_ref[0], masks_ref[2]
    low, high = jnp.minimum(first, third), jnp.maximum(first, third)
    low_bit, high_bit = jnp.int32(0), jnp.int32(0)
    for k in range(1, all_bits):
        low_bit += (low >= 1 << k).astype(jnp.int32)
        high_bit += (high >= 1 << k).astype(jnp.int32)
    before = low_bit * (all_bits - 1) - low_bit * (low_bit + 1) // 2
    index_ref[0] = before + high_bit - low_bit - 1
    for half, at, load in loads:
        load.wait()
        own_ref[half, pl.ds(at, ROWS), :] = wide[half, pl.ds(at, ROWS), :].astype(jnp.bfloat16)


def body(low_count, all_bits, images, texts, match, masks):
    low_bits = low_count.bit_length() - 1
    half, width = images.shape
    scale = 1.0 / (half * half * (masks.shape[0] + 1.0))
    smem = pl.BlockSpec(memory_space=pltpu.SMEM)
    anywhere = pl.BlockSpec(memory_space=pl.ANY)
    own, index = pl.pallas_call(
        partial(prepare, all_bits),
        out_shape=(pltpu.VMEM((2, half, width), jnp.bfloat16), pltpu.SMEM((1,), jnp.int32)),
        in_specs=[smem, anywhere, anywhere],
        out_specs=(pl.BlockSpec(memory_space=pltpu.VMEM), smem),
        scratch_shapes=[
            pltpu.VMEM((2, half, width), jnp.float32),
            pltpu.SemaphoreType.DMA((2, half // ROWS)),
        ],
        compiler_params=pltpu.CompilerParams(vmem_limit_bytes=16 * 2**20),
        name="prepare",
    )(*(pltpu.with_memory_space_constraint(x, pltpu.HBM) for x in (masks, images, texts)))
    sets = [
        (low, high, SECOND) for low in range(low_bits) for high in range(low + 1, all_bits - 1)
    ]
    branches = [
        partial(meet_call, bits, number, scale, low_count) for number, bits in enumerate(sets)
    ]
    return lax.switch(index[0], branches, own, match)


def solution(mesh):
    rows = P(("dx", "dy"), None)
    low_count = mesh.shape["dy"]
    all_bits = (low_count * mesh.shape["dx"]).bit_length() - 1
    return jax.shard_map(
        partial(body, low_count, all_bits),
        mesh=mesh,
        in_specs=(rows, rows, rows, P()),
        out_specs=(rows, rows, P(("dx", "dy"))),
        check_vma=False,
    )
```

```python
from functools import partial

import jax
import jax.numpy as jnp
from jax import lax
from jax.experimental import pallas as pl
from jax.experimental.pallas import tpu as pltpu
from jax.sharding import PartitionSpec as P

MESH = pl.DeviceIdType.MESH
BIAS = -2.0
SECOND = 8
WIDE = 384
ROWS = 64
PIECE = 32

LOAD = {0: 0.2, 1: 1, 2: 1.01, 3: 4, 4: 4.01, 5: 1, 6: 2, 7: 1, 8: 1.02}
HALFWAY, NEIGHBOUR = 4, 5
QUARTER, TURN = 3, 6
RELAYED = {(1, 2), (3, 4), (4, 5), (4, 6), (7, 8)}


def plan_for(bits, half_rows):
    def whole(bit, half):
        return half, [(bit, 0, 0, half_rows)]

    order = sorted(bits, key=lambda bit: LOAD[bit])
    pieces = half_rows // PIECE
    for pair in RELAYED:
        if set(pair) <= set(bits) and LOAD[order[-1]] < 2 * max(LOAD[bit] for bit in pair):
            near, far = sorted(pair, key=lambda bit: LOAD[bit])
            (other,) = set(bits) - set(pair)
            if LOAD[other] * 2 < LOAD[far]:
                uses = [(other, 0), (near, 0), (other, 1), (far, 0), (near, 1), (far, 1)]
                passed = [1, 2, 4, pieces, pieces + 4, pieces + 6, 2 * pieces, 2 * pieces]
            else:
                uses = [(near, 0), (other, 0), (far, 0), (near, 1), (other, 1), (far, 1)]
                passed = [1, 2, pieces, pieces + 2, pieces + 4, 2 * pieces, 2 * pieces, 2 * pieces]
            return near, far, [whole(*use) for use in uses], passed
    if order[-1] == HALFWAY:
        uses = [(bit, half) for part in (order[:-1], order[-1:]) for half in (0, 1) for bit in part]
        passed = [1, 2, 6, pieces, pieces + 4, pieces + 6, 2 * pieces, 2 * pieces]
        return NEIGHBOUR, HALFWAY, [whole(*use) for use in uses], passed
    light = [bit for bit in order if LOAD[bit] * 3 <= LOAD[order[-1]]]
    heavy = [bit for bit in order if bit not in light]
    tiles = [whole(bit, half) for bit in light for half in (0, 1)] + [whole(bit, 0) for bit in heavy]
    sent = dict.fromkeys(heavy, 0)
    for at in range(len(heavy)):
        parts, filled = [], 0
        for turn, bit in enumerate(heavy):
            rows = half_rows // len(heavy) // 16 * 16
            if turn == at:
                rows = half_rows - rows * (len(heavy) - 1)
            parts.append((bit, sent[bit], filled, rows))
            sent[bit] += rows
            filled += rows
        tiles.append((1, parts))
    return None, None, tiles, None


def flipped(index, mask):
    for k in range(16):
        if mask >> k & 1:
            step = 1 << k
            index = index + step * (1 - 2 * ((index // step) % 2))
    return index


def meet(bits, scale, low_count, *refs):
    (own_ref, match_ref, image_ref, text_ref, loss_ref, *refs) = refs
    (blocks, relay, labels, logits, g, losses, own_sem, send_sem, recv_sem, relay_sem, near_sem) = refs
    _, half_rows, width = own_ref.shape
    near, far, tiles, passed = plan_for(bits, half_rows)
    pieces = half_rows // PIECE
    dx, dy = lax.axis_index("dx"), lax.axis_index("dy")

    def device(mask):
        return (flipped(dx, mask // low_count), flipped(dy, mask % low_count))

    masks = {bit: 1 << bit for bit in bits}
    if far is not None:
        masks[near] = 1 << near
        masks[far] = 1 << near | 1 << far
    barrier = pltpu.get_barrier_semaphore()
    for mask in masks.values():
        pl.semaphore_signal(barrier, inc=1, device_id=device(mask), device_id_type=MESH)

    first_row = {(bit, half): 2 + k for k, (half, parts) in enumerate(tiles) for bit, *_ in parts}
    keep = pltpu.make_async_copy(own_ref, blocks.at[pl.ds(0, 2)], own_sem)
    keep.start()

    def part_copy(k, half, part):
        bit, start, row, rows = part
        return pltpu.make_async_remote_copy(
            src_ref=own_ref.at[half, pl.ds(start, rows)],
            dst_ref=blocks.at[k, pl.ds(row, rows)],
            send_sem=send_sem.at[k],
            recv_sem=recv_sem.at[k],
            device_id=device(masks[bit]),
            device_id_type=MESH,
        )

    def piece_copy(half, piece, forward):
        rows = pl.ds(pl.multiple_of(piece * PIECE, PIECE), PIECE)
        there = first_row[far, 0] + half * (first_row[far, 1] - first_row[far, 0])
        if near in bits:
            here = first_row[near, 0] + half * (first_row[near, 1] - first_row[near, 0])
            stop, sent = blocks.at[here, rows], send_sem.at[here]
        else:
            stop, sent = relay.at[half, rows], relay_sem.at[half]
        return pltpu.make_async_remote_copy(
            src_ref=stop if forward else own_ref.at[half, rows],
            dst_ref=blocks.at[there, rows] if forward else stop,
            send_sem=send_sem.at[there] if forward else sent,
            recv_sem=recv_sem.at[there] if forward else near_sem.at[half, piece],
            device_id=device(masks[far if forward else near]),
            device_id_type=MESH,
        )

    block = dx * low_count + dy
    second = (block // (1 << QUARTER)) % 2 == (block // (1 << TURN)) % 2
    turns = QUARTER in bits and near is None
    pl.semaphore_wait(barrier, len(masks))
    sends = [
        (half, -LOAD[part[0]], part[1], k, part)
        for k, (half, parts) in enumerate(tiles, 2)
        for part in parts
        if part[0] not in (near, far)
    ]
    for half in (0, 1):
        if near is not None:

            @pl.loop(0, pieces)
            def _(piece, half=half):
                piece_copy(half, piece, False).start()

        for _, _, _, k, part in sorted(send for send in sends if send[0] == half):
            if turns and part[0] == QUARTER:

                @pl.when(jnp.logical_not(second))
                def _(k=k, half=half, part=part):
                    part_copy(k, half, part).start()

            else:
                part_copy(k, half, part).start()

    @pl.loop(0, half_rows // ROWS)
    def _(step):
        rows = pl.ds(pl.multiple_of(step * ROWS, ROWS), ROWS)
        zero = jnp.zeros((ROWS, width), jnp.float32)
        image_ref[rows, :] = zero
        text_ref[rows, :] = zero

    square = (half_rows, half_rows)
    row = lax.broadcasted_iota(jnp.int32, square, 0)
    column = lax.broadcasted_iota(jnp.int32, square, 1)
    short = jnp.bfloat16
    hits = jnp.where(row == match_ref[...], 1.0, 0.0).astype(short)
    labels[1] = hits
    labels[0] = across(jnp.where(row == column, 1.0, 0.0).astype(short), hits).astype(short)
    labels[2] = jnp.zeros(square, short)
    losses[...] = jnp.zeros_like(losses)
    keep.wait()

    def chosen(k, numbers):
        return sum(((k == number).astype(jnp.int32) for number in numbers), jnp.int32(0))

    @pl.loop(0, 2 + len(tiles))
    def _(k):
        side = chosen(k, [1] + [at for at, (half, _) in enumerate(tiles, 2) if half == 1])

        if near is not None:
            low = sum((more - less) * (k > at).astype(jnp.int32) for at, (less, more) in enumerate(zip([0] + passed, passed)) if more > less)
            high = sum((more - less) * (k >= at).astype(jnp.int32) for at, (less, more) in enumerate(zip([0] + passed, passed)) if more > less)

            @pl.loop(low, high)
            def _(at):
                half = at // pieces
                piece = at - half * pieces
                piece_copy(half, piece, False).wait_recv()
                piece_copy(half, piece, True).start()

            waits = chosen(k, [at for at, (_, parts) in enumerate(tiles, 2) if parts[0][0] != near])
        else:
            waits = (k >= 2).astype(jnp.int32)

        logits[...] = jnp.full(square, BIAS, jnp.float32)

        @pl.when(k > len(tiles))
        def _():
            loss_ref[0] = jnp.sum(losses[...]) * scale

        @pl.when(waits == 1)
        def _():
            pltpu.make_async_copy(blocks.at[k], blocks.at[k], recv_sem.at[k]).wait()

        if turns:

            @pl.when(jnp.logical_and(second, k > len(tiles)))
            def _():
                for half, _, _, place, part in sends:
                    if part[0] == QUARTER:
                        part_copy(place, half, part).start()

        @pl.loop(0, width // WIDE)
        def _(step):
            columns = pl.ds(pl.multiple_of(step * WIDE, WIDE), WIDE)
            logits[...] += across(blocks[1 - side, :, columns], blocks[k, :, columns])

        @pl.loop(0, half_rows // ROWS)
        def _(step):
            rows = pl.ds(pl.multiple_of(step * ROWS, ROWS), ROWS)
            x = logits[rows, :]
            label = labels[jnp.minimum(k, 2), rows, :].astype(jnp.float32)
            e = jnp.exp(-jnp.abs(x))
            s = jnp.where(x >= 0, 1.0, e) / (1.0 + e)
            g[rows, :] = (s - label).astype(short)

        @pl.loop(0, (1 - side) * (half_rows // ROWS))
        def _(step):
            rows = pl.ds(pl.multiple_of(step * ROWS, ROWS), ROWS)
            x = logits[rows, :]
            label = labels[jnp.minimum(k, 2), rows, :].astype(jnp.float32)
            loss = jnp.maximum(jnp.where(label > 0, -x, x), 0.0) + jnp.log1p(jnp.exp(-jnp.abs(x)))
            losses[...] += jnp.sum(loss.reshape(ROWS // 8, 8, half_rows), axis=0)

        for number, grad_ref in enumerate((image_ref, text_ref)):

            @pl.loop(0, (side == number).astype(jnp.int32) * (width // WIDE))
            def _(step, grad_ref=grad_ref):
                columns = pl.ds(pl.multiple_of(step * WIDE, WIDE), WIDE)
                grad_ref[:, columns] += times(g[...], blocks[k, :, columns])

    @pl.loop(2, 2 + len(tiles))
    def _(k):
        pltpu.make_async_copy(own_ref.at[0], own_ref.at[0], send_sem.at[k]).wait()

    if near is not None and near not in bits:
        for half in (0, 1):
            pltpu.make_async_copy(own_ref.at[half], own_ref.at[half], relay_sem.at[half]).wait()


def meet_call(bits, number, scale, low_count, own, match):
    _, half, width = own.shape
    places = 2 + 2 * len(bits)
    vmem = pl.BlockSpec(memory_space=pltpu.VMEM)
    return pl.pallas_call(
        partial(meet, bits, scale, low_count),
        out_shape=(
            pltpu.VMEM((half, width), jnp.float32),
            pltpu.VMEM((half, width), jnp.float32),
            jax.ShapeDtypeStruct((1,), jnp.float32),
        ),
        in_specs=[vmem, vmem],
        out_specs=(vmem, vmem, pl.BlockSpec(memory_space=pltpu.SMEM)),
        scratch_shapes=[
            pltpu.VMEM((places, half, width), jnp.bfloat16),
            pltpu.VMEM((2, half, width), jnp.bfloat16),
            pltpu.VMEM((3, half, half), jnp.bfloat16),
            pltpu.VMEM((half, half), jnp.float32),
            pltpu.VMEM((half, half), jnp.bfloat16),
            pltpu.VMEM((8, half), jnp.float32),
            pltpu.SemaphoreType.DMA,
            pltpu.SemaphoreType.DMA((places,)),
            pltpu.SemaphoreType.DMA((places,)),
            pltpu.SemaphoreType.DMA((2,)),
            pltpu.SemaphoreType.DMA((2, half // PIECE)),
        ],
        compiler_params=pltpu.CompilerParams(
            collective_id=number, has_side_effects=True, vmem_limit_bytes=24 * 2**20
        ),
        cost_estimate=pl.CostEstimate(
            flops=32 * half * half * width, bytes_accessed=16 * half * width, transcendentals=0
        ),
        name="meet_" + "_".join(str(bit) for bit in bits),
    )(own, match)


def across(a, b):
    return lax.dot_general(a, b, (((1,), (1,)), ((), ())), preferred_element_type=jnp.float32)


def times(a, b):
    return jnp.dot(a, b, preferred_element_type=jnp.float32)


def prepare(all_bits, masks_ref, images_ref, texts_ref, own_ref, index_ref, wide, load_sem):
    half_rows = texts_ref.shape[0]
    loads = [
        (half, at, pltpu.make_async_copy(
            ref.at[pl.ds(at, ROWS)], wide.at[half, pl.ds(at, ROWS)], load_sem.at[half, at // ROWS]
        ))
        for half, ref in enumerate((texts_ref, images_ref))
        for at in range(0, half_rows, ROWS)
    ]
    for _, _, load in loads:
        load.start()
    first, third = masks_ref[0], masks_ref[2]
    low, high = jnp.minimum(first, third), jnp.maximum(first, third)
    low_bit, high_bit = jnp.int32(0), jnp.int32(0)
    for k in range(1, all_bits):
        low_bit += (low >= 1 << k).astype(jnp.int32)
        high_bit += (high >= 1 << k).astype(jnp.int32)
    before = low_bit * (all_bits - 1) - low_bit * (low_bit + 1) // 2
    index_ref[0] = before + high_bit - low_bit - 1
    for half, at, load in loads:
        load.wait()
        own_ref[half, pl.ds(at, ROWS), :] = wide[half, pl.ds(at, ROWS), :].astype(jnp.bfloat16)


def body(low_count, all_bits, images, texts, match, masks):
    low_bits = low_count.bit_length() - 1
    half, width = images.shape
    scale = 1.0 / (half * half * (masks.shape[0] + 1.0))
    smem = pl.BlockSpec(memory_space=pltpu.SMEM)
    anywhere = pl.BlockSpec(memory_space=pl.ANY)
    own, index = pl.pallas_call(
        partial(prepare, all_bits),
        out_shape=(pltpu.VMEM((2, half, width), jnp.bfloat16), pltpu.SMEM((1,), jnp.int32)),
        in_specs=[smem, anywhere, anywhere],
        out_specs=(pl.BlockSpec(memory_space=pltpu.VMEM), smem),
        scratch_shapes=[
            pltpu.VMEM((2, half, width), jnp.float32),
            pltpu.SemaphoreType.DMA((2, half // ROWS)),
        ],
        compiler_params=pltpu.CompilerParams(vmem_limit_bytes=16 * 2**20),
        name="prepare",
    )(*(pltpu.with_memory_space_constraint(x, pltpu.HBM) for x in (masks, images, texts)))
    sets = [
        (low, high, SECOND) for low in range(low_bits) for high in range(low + 1, all_bits - 1)
    ]
    branches = [
        partial(meet_call, bits, number, scale, low_count) for number, bits in enumerate(sets)
    ]
    return lax.switch(index[0], branches, own, match)


def solution(mesh):
    rows = P(("dx", "dy"), None)
    low_count = mesh.shape["dy"]
    all_bits = (low_count * mesh.shape["dx"]).bit_length() - 1
    return jax.shard_map(
        partial(body, low_count, all_bits),
        mesh=mesh,
        in_specs=(rows, rows, rows, P()),
        out_specs=(rows, rows, P(("dx", "dy"))),
        check_vma=False,
    )
```
